32 devices in a mesh: grp: 2 (over y), row: 4 (over z), col: 2 (over x), sub: 2 (over core).
Axes of the slice: x: 2, y: 2, z: 4, core: 2. Of those that a mesh axis runs over, the one named last changes fastest.
Arguments:
- cotangent: float32 [2048, 256], P(('grp', 'col', 'row'), 'sub'), parts along dimension 0, may hold values from -6 to 6
- node_inputs: bfloat16 [2048, 256], P(('grp', 'col', 'row'), 'sub'), parts along dimension 0, may hold values from -0.1875 to 0.1875
- tiles: bfloat16 [8, 2, 64, 128, 128], P(('grp', 'row'), 'col'), parts along dimension 0, may hold values from -0.109375 to 0.109375
- tile_rows: int32 [8, 2, 64], P(('grp', 'row'), 'col'), parts along dimension 0, may hold values from 0 to 3
- tile_cols: int32 [8, 2, 64], P(('grp', 'row'), 'col'), parts along dimension 0, may hold values from 0 to 1
- tile_counts: int32 [8, 2], P(('grp', 'row'), 'col'), parts along dimension 0, may hold values from 8 to 64, as said below
Outputs:
- node_grad: float32 [2048, 256], P(('grp', 'col', 'row'), 'sub'), parts along dimension 0
- weight_grad: float32 [512, 256], P('grp', 'sub'), parts along dimension 0
The draws below stay inside these ranges and needn't reach their ends.
There are 2 independent parts, one for each index of `grp`. The reference program is written for one: setup_inputs(seed, part) draws one part's arguments, and reference() takes and returns one part's arrays. A program takes and returns all parts, laid end to end along the dimension named above; each array names one. Nothing has to cross between parts.
Inputs may be any that keep to these rules, and one draw needn't show every extreme that they name: Slots 0 to tile_counts - 1 of a row and column index are live, the others are ignored; in every part some index has all 64 slots live.
All inputs are finite; a program needn't handle non-finite values.
Results may differ from the reference program's by a relative error of at most 0.025.
Values may be sent and summed in bfloat16 or wider, within the bound.
A program may use at most 64 MiB of HBM per device.

```python
import jax
import jax.numpy as jnp
from jax import lax

FEATURES = 256
TILE_SIZE = 128
PROP_STEPS = 4
TILE_SLOTS = 64
PIECE_ROWS = 128
NODES = 1024
BLOCK_TILES = 4
INPUT_TILES = 2
N_ROW = 4
N_COL = 2


def draw_tile_counts(key, part):
    key = jax.random.fold_in(key, 7)
    count_key, peak_key = jax.random.split(key)
    spread = TILE_SLOTS - 8
    uniform_draw = jax.random.randint(count_key, (N_ROW * N_COL,), 0, spread + 1)
    counts = 8 + uniform_draw * uniform_draw // spread
    chosen = jax.random.randint(peak_key, (), 0, N_ROW * N_COL)
    counts = jnp.where(jnp.arange(N_ROW * N_COL) == chosen, TILE_SLOTS, counts)
    return counts.reshape(N_ROW, N_COL).astype(jnp.int32)


def place_ends(array, own_key, smallest, top_value):
    longest = array.shape.index(max(array.shape))
    spots = []
    for shift in (0, 1):
        where = [jax.random.randint(jax.random.fold_in(own_key, axis), (), 0, length) for axis, length in enumerate(array.shape)]
        where[longest] = (where[longest] + shift) % array.shape[longest]
        spots.append(tuple(where))
    return array.at[spots[0]].set(smallest).at[spots[1]].set(top_value)


def block_scale(stream_key, dims, cuts, low, high):
    loudness = 1.0
    for dim, shards_of in cuts:
        steps = jax.random.uniform(jax.random.fold_in(jax.random.fold_in(stream_key, 6), dim), (shards_of,), jnp.float32, low / len(cuts), high / len(cuts))
        loudness = loudness * jnp.repeat(jnp.exp(steps), dims[dim] // shards_of).reshape((-1,) + (1,) * (len(dims) - 1 - dim))
    return loudness


def normal_values(stream_key, shape, deviation, reach, shards=(), kind=jnp.bfloat16):
    drawn = jax.random.normal(stream_key, shape, jnp.float32) * deviation
    if len(shards) > 0:
        drawn = block_scale(stream_key, shape, shards, -0.22, 0.18) * drawn
    return jnp.clip(drawn, min=-reach, max=reach).astype(kind)


def setup_inputs(seed: int = 0, part: int = 0) -> dict:
    keys = jax.random.split(jax.random.key(seed), 7)
    part_keys = jax.random.split(jax.random.fold_in(keys[6], part), 7)
    return {
        "cotangent": normal_values(part_keys[0], (NODES, FEATURES), 1.0, 6.0, ((0, 8), (1, 2)), jnp.float32),
        "node_inputs": normal_values(part_keys[1], (NODES, FEATURES), (NODES ** -0.5), 0.1875, ((0, 8), (1, 2))),
        "tiles": normal_values(part_keys[2], (N_ROW, N_COL, TILE_SLOTS, TILE_SIZE, TILE_SIZE), ((8 + (TILE_SLOTS - 8) // 3) * TILE_SIZE * TILE_SIZE // PIECE_ROWS) ** -0.5, 0.109375, ((0, 4), (1, 2))),
        "tile_rows": place_ends(jax.random.randint(part_keys[3], (N_ROW, N_COL, TILE_SLOTS), 0, BLOCK_TILES), jax.random.fold_in(part_keys[3], 1), 0, BLOCK_TILES - 1).astype(jnp.int32),
        "tile_cols": place_ends(jax.random.randint(part_keys[4], (N_ROW, N_COL, TILE_SLOTS), 0, INPUT_TILES), jax.random.fold_in(part_keys[4], 1), 0, INPUT_TILES - 1).astype(jnp.int32),
        "tile_counts": draw_tile_counts(jax.random.fold_in(jax.random.fold_in(keys[6], part), 71), part),
    }


teleport = 0.1


def propagate(sent, tiles, tile_rows, tile_cols, tile_counts):
    block_tiles = N_ROW * PIECE_ROWS // TILE_SIZE
    input_tiles = N_COL * PIECE_ROWS // TILE_SIZE
    pieces = jnp.swapaxes(sent.reshape(N_COL, N_ROW, PIECE_ROWS, FEATURES), 0, 1)
    column_index = jnp.broadcast_to(jnp.arange(N_COL)[:, None], (N_COL, TILE_SLOTS))

    def add_device_row(totals, inputs):
        pieces_row, tiles_row, rows_row, cols_row, counts_row = inputs
        live_slots = (jnp.arange(TILE_SLOTS)[None, :] < counts_row[:, None]).astype(jnp.float32)
        masked = tiles_row.astype(jnp.float32) * live_slots[:, :, None, None]
        dense = jnp.zeros((N_COL, block_tiles, input_tiles, TILE_SIZE, TILE_SIZE), jnp.float32)
        dense = dense.at[column_index, rows_row, cols_row].add(masked)
        stacked = pieces_row.reshape(input_tiles, TILE_SIZE, FEATURES).astype(jnp.float32)
        partial_value = jnp.einsum("cbtij,tjf->cbif", dense, stacked, precision=lax.Precision.HIGHEST)
        rounded = lax.optimization_barrier(partial_value.astype(jnp.bfloat16))
        return totals + rounded.astype(jnp.float32).reshape(N_COL, N_ROW * PIECE_ROWS, FEATURES), None

    start_totals = jnp.zeros((N_COL, N_ROW * PIECE_ROWS, FEATURES), jnp.float32)
    totals, unused = lax.scan(add_device_row, start_totals, (pieces, tiles, tile_rows, tile_cols, tile_counts))
    return totals.reshape(N_COL * N_ROW * PIECE_ROWS, FEATURES)


def reference(cotangent, node_inputs, tiles, tile_rows, tile_cols, tile_counts):
    adjoint = cotangent.astype(jnp.float32)
    node_grad = jnp.zeros_like(adjoint)
    for iteration in range(PROP_STEPS):
        node_grad = node_grad + teleport * adjoint
        sent = adjoint.astype(jnp.bfloat16)
        adjoint = (1.0 - teleport) * propagate(sent, tiles, tile_rows, tile_cols, tile_counts)
    node_grad = node_grad + adjoint
    weight_grad = jnp.dot(node_inputs.astype(jnp.float32).T, node_grad, precision=lax.Precision.HIGHEST)
    return (node_grad, weight_grad)
```

```python
import functools

import jax
import jax.numpy as jnp
from jax import lax
from jax.experimental import pallas as pl
from jax.experimental.pallas import tpu as pltpu
from jax.sharding import PartitionSpec as P

PROP_STEPS = 4


teleport = 0.1

MESH = pl.DeviceIdType.MESH
LOCAL_BYTES = 8 * 1024 * 1024


def tile_products(stacked, live_tiles, own_rows, own_cols, block_tiles):
    chosen = jnp.take(stacked, own_cols, axis=0)
    products = jnp.einsum("sij,sjf->sif", live_tiles, chosen, preferred_element_type=jnp.float32)
    return jax.ops.segment_sum(products, own_rows, num_segments=block_tiles)


def exchange_body(cotangent, node_inputs, tiles, tile_rows, tile_cols, tile_counts):
    own_tiles = tiles[0, 0]
    own_rows = tile_rows[0, 0]
    own_cols = tile_cols[0, 0]
    own_count = tile_counts[0, 0]
    piece_rows, half_width = cotangent.shape
    slot_count = own_tiles.shape[0]
    tile_size = own_tiles.shape[1]
    row_devices = lax.axis_size("row")
    block_tiles = row_devices * piece_rows // tile_size
    live_mask = (jnp.arange(slot_count) < own_count).astype(jnp.bfloat16)
    live_tiles = own_tiles * live_mask[:, None, None]
    adjoint = cotangent
    node_grad = jnp.zeros_like(cotangent)
    for iteration in range(PROP_STEPS):
        node_grad = node_grad + teleport * adjoint
        sent = adjoint.astype(jnp.bfloat16)
        gathered = lax.all_gather(sent, "col", axis=0, tiled=True)
        stacked = gathered.reshape(-1, tile_size, half_width)
        partial_value = tile_products(stacked, live_tiles, own_rows, own_cols, block_tiles)
        rounded = lax.optimization_barrier(
            partial_value.reshape(block_tiles * tile_size, half_width).astype(jnp.bfloat16)
        )
        received = lax.all_to_all(
            rounded.reshape(row_devices, piece_rows, half_width),
            "row",
            split_axis=0,
            concat_axis=0,
            tiled=True,
        )
        summed = jnp.sum(received.astype(jnp.float32), axis=0)
        adjoint = (1.0 - teleport) * summed
    node_grad = node_grad + adjoint
    full_inputs = lax.all_gather(node_inputs, "sub", axis=1, tiled=True)
    terms = jnp.dot(full_inputs.astype(jnp.float32).T, node_grad, precision=lax.Precision.HIGHEST)
    weight_grad = lax.psum(terms, ("row", "col"))
    return (node_grad, weight_grad)


def densify_kernel(chunk, rows_ref, cols_ref, count_ref, tiles_ref, out_ref, slots, totals, sems):
    slot_count, half, tile = slots.shape
    block_tiles = out_ref.shape[0] // half
    input_tiles = out_ref.shape[1] // tile
    first = pl.multiple_of(lax.axis_index("sub") * half, half)
    count = count_ref[0, 0]
    copies = []
    for k in range(slot_count // chunk):
        copies.append(
            pltpu.make_async_copy(
                tiles_ref.at[0, 0, pl.ds(k * chunk, chunk), pl.ds(first, half), :],
                slots.at[pl.ds(k * chunk, chunk)],
                sems.at[k],
            )
        )
        copies[-1].start()
    totals[...] = jnp.zeros_like(totals)

    def add_slot(slot, carry):
        place = rows_ref[0, 0, slot] * input_tiles + cols_ref[0, 0, slot]
        totals[place] += slots[slot].astype(jnp.float32)
        return carry

    for k in range(slot_count // chunk):
        copies[k].wait()
        lax.fori_loop(k * chunk, jnp.minimum(count, (k + 1) * chunk), add_slot, 0)
    for b in range(block_tiles):
        for t in range(input_tiles):
            out_ref[b * half : (b + 1) * half, t * tile : (t + 1) * tile] = totals[b * input_tiles + t].astype(
                jnp.bfloat16
            )


def gather_kernel(
    n_row,
    dense_ref,
    cot_ref,
    inputs_ref,
    grad_ref,
    weight_ref,
    mat,
    states,
    feats,
    total,
    sem_send,
    sem_z,
    sem_x,
    sem_sib,
):
    c = lax.axis_index("col")
    r = lax.axis_index("row")
    h = lax.axis_index("sub")
    oc = 1 - c
    oh = 1 - h
    piece = cot_ref.shape[0]
    half = piece // 2
    has_up = r < n_row - 1
    has_down = r > 0
    up = {"row": r + 1}
    down = {"row": r - 1}
    across = {"col": oc}
    sibling = {"sub": oh}

    def place(kind, col, row, core):
        if kind == 0:
            return states.at[0, row, pl.ds(pl.multiple_of(col * piece, piece), piece), :]
        if kind == 1:
            return mat.at[col, core, row]
        return feats.at[col, core, row]

    def remote(kind, col, row, core, link, sem, device):
        ref = place(kind, col, row, core)
        return pltpu.make_async_remote_copy(
            src_ref=ref,
            dst_ref=ref,
            send_sem=sem_send.at[kind, link, col, row],
            recv_sem=sem,
            device_id=device,
            device_id_type=MESH,
        )

    def to_up(kind, row):
        return remote(kind, c, row, h, 0, sem_z.at[kind, row], up)

    def to_down(kind, row):
        return remote(kind, c, row, h, 1, sem_z.at[kind, row], down)

    def to_across(kind, row):
        return remote(kind, c, row, h, 2, sem_x.at[kind, row], across)

    def to_sibling(kind, col, row):
        return remote(kind, col, row, h, 3, sem_sib.at[kind, col, row], sibling)

    def from_z(kind, row):
        return remote(kind, c, row, h, 0, sem_z.at[kind, row], across)

    def from_across(kind, row):
        return remote(kind, oc, row, h, 2, sem_x.at[kind, row], across)

    def from_sibling(kind, col, row):
        return remote(kind, col, row, oh, 3, sem_sib.at[kind, col, row], sibling)

    barrier = pltpu.get_barrier_semaphore()
    pl.semaphore_signal(barrier, inc=1, device_id=across, device_id_type=MESH)
    pl.semaphore_signal(barrier, inc=1, device_id=sibling, device_id_type=MESH)

    @pl.when(has_up)
    def _():
        pl.semaphore_signal(barrier, inc=1, device_id=up, device_id_type=MESH)

    @pl.when(has_down)
    def _():
        pl.semaphore_signal(barrier, inc=1, device_id=down, device_id_type=MESH)

    states[0, r, pl.ds(pl.multiple_of(c * piece, piece), piece), :] = cot_ref[...].astype(jnp.bfloat16)
    mat[c, h, r] = dense_ref[...]
    feats[c, h, r] = inputs_ref[...]

    pl.semaphore_wait(barrier, 2 + has_up.astype(jnp.int32) + has_down.astype(jnp.int32))

    def spread(kind, row, go_up, go_down):
        if go_up:
            @pl.when(has_up)
            def _():
                to_up(kind, row).start()
        if go_down:
            @pl.when(has_down)
            def _():
                to_down(kind, row).start()
        to_across(kind, row).start()
        if kind > 0:
            to_sibling(kind, c, row).start()

    def arrivals(kinds):
        for kind in kinds:
            spread(kind, r, True, True)
        for d in range(n_row):
            if d > 0:
                for kind in kinds:
                    @pl.when(r >= d)
                    def _():
                        from_z(kind, r - d).wait_recv()
                        spread(kind, r - d, True, False)

                    @pl.when(r + d < n_row)
                    def _():
                        from_z(kind, r + d).wait_recv()
                        spread(kind, r + d, False, True)
            for kind in kinds:
                def crossed(row):
                    from_across(kind, row).wait_recv()
                    if kind > 0:
                        to_sibling(kind, oc, row).start()

                if d == 0:
                    crossed(r)
                else:
                    @pl.when(r >= d)
                    def _():
                        crossed(r - d)

                    @pl.when(r + d < n_row)
                    def _():
                        crossed(r + d)

    arrivals((0, 1))
    arrivals((2,))

    for col in range(2):
        for row in range(n_row):
            from_sibling(1, col, row).wait_recv()

    for step in range(PROP_STEPS):
        now = 0 if step == 0 else 1 + (step - 1) % 2
        later = 1 + step % 2
        last = step == PROP_STEPS - 1
        for col in range(2):
            for core in range(2):
                out = jnp.dot(mat[col, core, 0], states[now, 0], preferred_element_type=jnp.float32)
                for row in range(1, n_row):
                    out += jnp.dot(mat[col, core, row], states[now, row], preferred_element_type=jnp.float32)
                out = out * (1.0 - teleport)
                for row in range(n_row):
                    rows = slice(col * piece + core * half, col * piece + core * half + half)
                    part = out[row * half : (row + 1) * half]
                    if step == 0:
                        total[row, rows, :] = teleport * (states[0, row, rows, :].astype(jnp.float32) + part)
                    elif last:
                        total[row, rows, :] += part
                    else:
                        total[row, rows, :] += teleport * part
                    if not last:
                        states[later, row, rows, :] = part.astype(jnp.bfloat16)

    own = cot_ref[...]
    own_rows = pl.ds(pl.multiple_of(c * piece, piece), piece)
    grad = total[r, own_rows, :] + teleport * (own - own.astype(jnp.bfloat16).astype(jnp.float32))
    total[r, own_rows, :] = grad
    grad_ref[...] = grad

    for col in range(2):
        for row in range(n_row):
            from_sibling(2, col, row).wait_recv()

    width = inputs_ref.shape[1]
    for core in range(2):
        weight = jnp.zeros((width, cot_ref.shape[1]), jnp.float32)
        for col in range(2):
            for row in range(n_row):
                weight += lax.dot_general(
                    feats[col, core, row],
                    total[row, col * piece : (col + 1) * piece, :].astype(jnp.bfloat16),
                    (((0,), (0,)), ((), ())),
                    preferred_element_type=jnp.float32,
                )
        weight_ref[core * width : (core + 1) * width, :] = weight

    for kind in range(3):
        for row in range(n_row):
            to_across(kind, row).wait_send()

            @pl.when((row <= r) & has_up)
            def _():
                to_up(kind, row).wait_send()

            @pl.when((row >= r) & has_down)
            def _():
                to_down(kind, row).wait_send()

            if kind > 0:
                for col in range(2):
                    to_sibling(kind, col, row).wait_send()


def local_body(cotangent, node_inputs, tiles, tile_rows, tile_cols, tile_counts):
    piece, width = cotangent.shape
    slot_count, tile = tiles.shape[2], tiles.shape[3]
    n_row = lax.axis_size("row")
    half = tile // 2
    chunk = 8 if slot_count % 8 == 0 else slot_count
    smem = pl.BlockSpec(memory_space=pltpu.SMEM)
    vmem = pl.BlockSpec(memory_space=pltpu.VMEM)
    dense = pl.pallas_call(
        functools.partial(densify_kernel, chunk),
        out_shape=jax.ShapeDtypeStruct((n_row * half, 2 * tile), jnp.bfloat16),
        in_specs=[smem, smem, smem, pl.BlockSpec(memory_space=pl.ANY)],
        out_specs=vmem,
        scratch_shapes=[
            pltpu.VMEM((slot_count, half, tile), jnp.bfloat16),
            pltpu.VMEM((n_row * 2, half, tile), jnp.float32),
            pltpu.SemaphoreType.DMA((slot_count // chunk,)),
        ],
        compiler_params=pltpu.CompilerParams(vmem_limit_bytes=16 * 1024 * 1024),
        name="densify",
    )(tile_rows, tile_cols, tile_counts, tiles)
    return pl.pallas_call(
        functools.partial(gather_kernel, n_row),
        out_shape=(
            jax.ShapeDtypeStruct((piece, width), jnp.float32),
            jax.ShapeDtypeStruct((2 * node_inputs.shape[1], width), jnp.float32),
        ),
        in_specs=[vmem, vmem, vmem],
        out_specs=(vmem, vmem),
        scratch_shapes=[
            pltpu.VMEM((2, 2, n_row, n_row * half, 2 * tile), jnp.bfloat16),
            pltpu.VMEM((3, n_row, 2 * piece, width), jnp.bfloat16),
            pltpu.VMEM((2, 2, n_row, piece, node_inputs.shape[1]), jnp.bfloat16),
            pltpu.VMEM((n_row, 2 * piece, width), jnp.float32),
            pltpu.SemaphoreType.DMA((3, 4, 2, n_row)),
            pltpu.SemaphoreType.DMA((3, n_row)),
            pltpu.SemaphoreType.DMA((3, n_row)),
            pltpu.SemaphoreType.DMA((3, 2, n_row)),
        ],
        compiler_params=pltpu.CompilerParams(
            collective_id=0, has_side_effects=True, vmem_limit_bytes=32 * 1024 * 1024
        ),
        name="gather_steps",
    )(dense, cotangent, node_inputs)


def body(cotangent, node_inputs, tiles, tile_rows, tile_cols, tile_counts):
    nodes = lax.axis_size("row") * lax.axis_size("col") * cotangent.shape[0]
    fits = nodes * nodes * tiles.dtype.itemsize <= LOCAL_BYTES
    pairs = lax.axis_size("col") == 2 and lax.axis_size("sub") == 2
    whole_tiles = cotangent.shape[0] == tiles.shape[3] and tiles.shape[3] % 32 == 0
    chosen = local_body if fits and pairs and whole_tiles else exchange_body
    return chosen(cotangent, node_inputs, tiles, tile_rows, tile_cols, tile_counts)


def solution(mesh):
    in_specs = (
        P(("grp", "col", "row"), "sub"),
        P(("grp", "col", "row"), "sub"),
        P(("grp", "row"), "col", None, None, None),
        P(("grp", "row"), "col", None),
        P(("grp", "row"), "col", None),
        P(("grp", "row"), "col"),
    )
    out_specs = (P(("grp", "col", "row"), "sub"), P("grp", "sub"))
    return jax.shard_map(body, mesh=mesh, in_specs=in_specs, out_specs=out_specs, check_vma=False)
```

```python
import functools

import jax
import jax.numpy as jnp
from jax import lax
from jax.experimental import pallas as pl
from jax.experimental.pallas import tpu as pltpu
from jax.sharding import PartitionSpec as P

PROP_STEPS = 4


teleport = 0.1

MESH = pl.DeviceIdType.MESH
LOCAL_BYTES = 8 * 1024 * 1024
PIECES = 4


def tile_products(stacked, live_tiles, own_rows, own_cols, block_tiles):
    chosen = jnp.take(stacked, own_cols, axis=0)
    products = jnp.einsum("sij,sjf->sif", live_tiles, chosen, preferred_element_type=jnp.float32)
    return jax.ops.segment_sum(products, own_rows, num_segments=block_tiles)


def exchange_body(cotangent, node_inputs, tiles, tile_rows, tile_cols, tile_counts):
    own_tiles = tiles[0, 0]
    own_rows = tile_rows[0, 0]
    own_cols = tile_cols[0, 0]
    own_count = tile_counts[0, 0]
    piece_rows, half_width = cotangent.shape
    slot_count = own_tiles.shape[0]
    tile_size = own_tiles.shape[1]
    row_devices = lax.axis_size("row")
    block_tiles = row_devices * piece_rows // tile_size
    live_mask = (jnp.arange(slot_count) < own_count).astype(jnp.bfloat16)
    live_tiles = own_tiles * live_mask[:, None, None]
    adjoint = cotangent
    node_grad = jnp.zeros_like(cotangent)
    for iteration in range(PROP_STEPS):
        node_grad = node_grad + teleport * adjoint
        sent = adjoint.astype(jnp.bfloat16)
        gathered = lax.all_gather(sent, "col", axis=0, tiled=True)
        stacked = gathered.reshape(-1, tile_size, half_width)
        partial_value = tile_products(stacked, live_tiles, own_rows, own_cols, block_tiles)
        rounded = lax.optimization_barrier(
            partial_value.reshape(block_tiles * tile_size, half_width).astype(jnp.bfloat16)
        )
        received = lax.all_to_all(
            rounded.reshape(row_devices, piece_rows, half_width),
            "row",
            split_axis=0,
            concat_axis=0,
            tiled=True,
        )
        summed = jnp.sum(received.astype(jnp.float32), axis=0)
        adjoint = (1.0 - teleport) * summed
    node_grad = node_grad + adjoint
    full_inputs = lax.all_gather(node_inputs, "sub", axis=1, tiled=True)
    terms = jnp.dot(full_inputs.astype(jnp.float32).T, node_grad, precision=lax.Precision.HIGHEST)
    weight_grad = lax.psum(terms, ("row", "col"))
    return (node_grad, weight_grad)


def densify_kernel(chunk, rows_ref, cols_ref, count_ref, tiles_ref, out_ref, slots, totals, sems):
    slot_count, half, tile = slots.shape
    block_tiles = out_ref.shape[0] // half
    input_tiles = out_ref.shape[1] // tile
    first = pl.multiple_of(lax.axis_index("sub") * half, half)
    count = count_ref[0, 0]
    copies = []
    for k in range(slot_count // chunk):
        copies.append(
            pltpu.make_async_copy(
                tiles_ref.at[0, 0, pl.ds(k * chunk, chunk), pl.ds(first, half), :],
                slots.at[pl.ds(k * chunk, chunk)],
                sems.at[k],
            )
        )
        copies[-1].start()
    totals[...] = jnp.zeros_like(totals)

    def add_slot(slot, carry):
        place = rows_ref[0, 0, slot] * input_tiles + cols_ref[0, 0, slot]
        totals[place] += slots[slot].astype(jnp.float32)
        return carry

    for k in range(slot_count // chunk):
        copies[k].wait()
        lax.fori_loop(k * chunk, jnp.minimum(count, (k + 1) * chunk), add_slot, 0)
    for b in range(block_tiles):
        for t in range(input_tiles):
            out_ref[b * half : (b + 1) * half, t * tile : (t + 1) * tile] = totals[b * input_tiles + t].astype(
                jnp.bfloat16
            )


def gather_kernel(
    n_row,
    dense_ref,
    cot_ref,
    inputs_ref,
    grad_ref,
    weight_ref,
    mat,
    states,
    feats,
    total,
    sem_send,
    sem_z,
    sem_x,
    sem_sib,
):
    c = lax.axis_index("col")
    r = lax.axis_index("row")
    h = lax.axis_index("sub")
    oc = 1 - c
    oh = 1 - h
    piece = cot_ref.shape[0]
    half = piece // 2
    span = dense_ref.shape[0] // PIECES
    has_up = r < n_row - 1
    has_down = r > 0
    up = {"row": r + 1}
    down = {"row": r - 1}
    across = {"col": oc}
    sibling = {"sub": oh}

    def place(kind, col, row, core, p):
        if kind == 0:
            return states.at[0, row, pl.ds(pl.multiple_of(col * piece, piece), piece), :]
        if kind == 1:
            return mat.at[col, core, row, pl.ds(pl.multiple_of(p * span, span), span), :]
        return feats.at[col, core, row]

    def remote(kind, col, row, core, p, link, sems, device):
        ref = place(kind, col, row, core, p)
        slot = (0, 1 + p, 1 + PIECES)[kind]
        recv = sems.at[slot, row] if link < 3 else sems.at[slot, col, row]
        return pltpu.make_async_remote_copy(
            src_ref=ref,
            dst_ref=ref,
            send_sem=sem_send.at[slot, link, col, row],
            recv_sem=recv,
            device_id=device,
            device_id_type=MESH,
        )

    def to_up(kind, row, p=0):
        return remote(kind, c, row, h, p, 0, sem_z, up)

    def to_down(kind, row, p=0):
        return remote(kind, c, row, h, p, 1, sem_z, down)

    def to_across(kind, row, p=0):
        return remote(kind, c, row, h, p, 2, sem_x, across)

    def to_sibling(kind, col, row, p=0):
        return remote(kind, col, row, h, p, 3, sem_sib, sibling)

    def from_z(kind, row, p=0):
        return remote(kind, c, row, h, p, 0, sem_z, across)

    def from_across(kind, row, p=0):
        return remote(kind, oc, row, h, p, 2, sem_x, across)

    def from_sibling(kind, col, row, p=0):
        return remote(kind, col, row, oh, p, 3, sem_sib, sibling)

    def each_piece(act):
        def at_piece(p, carry):
            act(p)
            return carry

        lax.fori_loop(0, PIECES, at_piece, 0)

    barrier = pltpu.get_barrier_semaphore()
    pl.semaphore_signal(barrier, inc=1, device_id=across, device_id_type=MESH)
    pl.semaphore_signal(barrier, inc=1, device_id=sibling, device_id_type=MESH)

    @pl.when(has_up)
    def _():
        pl.semaphore_signal(barrier, inc=1, device_id=up, device_id_type=MESH)

    @pl.when(has_down)
    def _():
        pl.semaphore_signal(barrier, inc=1, device_id=down, device_id_type=MESH)

    states[0, r, pl.ds(pl.multiple_of(c * piece, piece), piece), :] = cot_ref[...].astype(jnp.bfloat16)
    mat[c, h, r] = dense_ref[...]
    feats[c, h, r] = inputs_ref[...]

    pl.semaphore_wait(barrier, 2 + has_up.astype(jnp.int32) + has_down.astype(jnp.int32))

    def spread(kind, row, go_up, go_down, p=0):
        if go_up:
            @pl.when(has_up)
            def _():
                to_up(kind, row, p).start()
        if go_down:
            @pl.when(has_down)
            def _():
                to_down(kind, row, p).start()
        if kind < 2:
            to_across(kind, row, p).start()
        if kind > 0:
            to_sibling(kind, c, row, p).start()

    def from_both(kind, d, p=0):
        @pl.when(r >= d)
        def _():
            from_z(kind, r - d, p).wait_recv()
            spread(kind, r - d, True, False, p)

        @pl.when(r + d < n_row)
        def _():
            from_z(kind, r + d, p).wait_recv()
            spread(kind, r + d, False, True, p)

    def crossed(kind, row, p=0):
        from_across(kind, row, p).wait_recv()
        if kind > 0:
            to_sibling(kind, oc, row, p).start()

    def crossed_both(d):
        if d == 0:
            crossed(0, r)
            each_piece(lambda p: crossed(1, r, p))
            return

        @pl.when(r >= d)
        def _():
            crossed(0, r - d)

        @pl.when(r + d < n_row)
        def _():
            crossed(0, r + d)

        def at_piece(p):
            @pl.when(r >= d)
            def _():
                crossed(1, r - d, p)

            @pl.when(r + d < n_row)
            def _():
                crossed(1, r + d, p)

        each_piece(at_piece)

    spread(0, r, True, True)
    each_piece(lambda p: spread(1, r, True, True, p))
    spread(2, r, True, True)
    for d in range(1, n_row):
        from_both(0, d)
        each_piece(lambda p: from_both(1, d, p))
        from_both(2, d)
        if d == 1:
            crossed_both(0)
    for row in range(n_row):
        to_across(2, row).start()
    for d in range(1, n_row):
        crossed_both(d)

    for col in range(2):
        for row in range(n_row):
            each_piece(lambda p: from_sibling(1, col, row, p).wait_recv())

    for step in range(PROP_STEPS):
        now = 0 if step == 0 else 1 + (step - 1) % 2
        later = 1 + step % 2
        last = step == PROP_STEPS - 1
        if last:
            for row in range(n_row):
                crossed(2, row)

        def block(index, carry):
            col, core = index // 2, index % 2
            out = jnp.dot(mat[col, core, 0], states[now, 0], preferred_element_type=jnp.float32)
            for row in range(1, n_row):
                out += jnp.dot(mat[col, core, row], states[now, row], preferred_element_type=jnp.float32)
            out = out * (1.0 - teleport)
            rows = pl.ds(pl.multiple_of(index * half, half), half)
            for row in range(n_row):
                part = out[row * half : (row + 1) * half]
                if step == 0:
                    total[row, rows, :] = teleport * (states[0, row, rows, :].astype(jnp.float32) + part)
                elif last:
                    total[row, rows, :] += part
                else:
                    total[row, rows, :] += teleport * part
                if not last:
                    states[later, row, rows, :] = part.astype(jnp.bfloat16)
            return carry

        lax.fori_loop(0, 4, block, 0)

    own = cot_ref[...]
    own_rows = pl.ds(pl.multiple_of(c * piece, piece), piece)
    grad = total[r, own_rows, :] + teleport * (own - own.astype(jnp.bfloat16).astype(jnp.float32))
    total[r, own_rows, :] = grad
    grad_ref[...] = grad

    for col in range(2):
        for row in range(n_row):
            from_sibling(2, col, row).wait_recv()

    width = inputs_ref.shape[1]
    for core in range(2):
        weight = jnp.zeros((width, cot_ref.shape[1]), jnp.float32)
        for col in range(2):
            for row in range(n_row):
                weight += lax.dot_general(
                    feats[col, core, row],
                    total[row, col * piece : (col + 1) * piece, :].astype(jnp.bfloat16),
                    (((0,), (0,)), ((), ())),
                    preferred_element_type=jnp.float32,
                )
        weight_ref[core * width : (core + 1) * width, :] = weight

    def sent(kind, row, p=0):
        to_across(kind, row, p).wait_send()

        @pl.when((row <= r) & has_up)
        def _():
            to_up(kind, row, p).wait_send()

        @pl.when((row >= r) & has_down)
        def _():
            to_down(kind, row, p).wait_send()

        if kind > 0:
            for col in range(2):
                to_sibling(kind, col, row, p).wait_send()

    def all_sent(row, carry):
        sent(0, row)
        each_piece(lambda p: sent(1, row, p))
        sent(2, row)
        return carry

    lax.fori_loop(0, n_row, all_sent, 0)


def local_body(cotangent, node_inputs, tiles, tile_rows, tile_cols, tile_counts):
    piece, width = cotangent.shape
    slot_count, tile = tiles.shape[2], tiles.shape[3]
    n_row = lax.axis_size("row")
    half = tile // 2
    chunk = 8 if slot_count % 8 == 0 else slot_count
    smem = pl.BlockSpec(memory_space=pltpu.SMEM)
    vmem = pl.BlockSpec(memory_space=pltpu.VMEM)
    dense = pl.pallas_call(
        functools.partial(densify_kernel, chunk),
        out_shape=jax.ShapeDtypeStruct((n_row * half, 2 * tile), jnp.bfloat16),
        in_specs=[smem, smem, smem, pl.BlockSpec(memory_space=pl.ANY)],
        out_specs=vmem,
        scratch_shapes=[
            pltpu.VMEM((slot_count, half, tile), jnp.bfloat16),
            pltpu.VMEM((n_row * 2, half, tile), jnp.float32),
            pltpu.SemaphoreType.DMA((slot_count // chunk,)),
        ],
        compiler_params=pltpu.CompilerParams(vmem_limit_bytes=16 * 1024 * 1024),
        name="densify",
    )(tile_rows, tile_cols, tile_counts, tiles)
    return pl.pallas_call(
        functools.partial(gather_kernel, n_row),
        out_shape=(
            jax.ShapeDtypeStruct((piece, width), jnp.float32),
            jax.ShapeDtypeStruct((2 * node_inputs.shape[1], width), jnp.float32),
        ),
        in_specs=[vmem, vmem, vmem],
        out_specs=(vmem, vmem),
        scratch_shapes=[
            pltpu.VMEM((2, 2, n_row, n_row * half, 2 * tile), jnp.bfloat16),
            pltpu.VMEM((3, n_row, 2 * piece, width), jnp.bfloat16),
            pltpu.VMEM((2, 2, n_row, piece, node_inputs.shape[1]), jnp.bfloat16),
            pltpu.VMEM((n_row, 2 * piece, width), jnp.float32),
            pltpu.SemaphoreType.DMA((2 + PIECES, 4, 2, n_row)),
            pltpu.SemaphoreType.DMA((2 + PIECES, n_row)),
            pltpu.SemaphoreType.DMA((2 + PIECES, n_row)),
            pltpu.SemaphoreType.DMA((2 + PIECES, 2, n_row)),
        ],
        compiler_params=pltpu.CompilerParams(
            collective_id=0, has_side_effects=True, vmem_limit_bytes=32 * 1024 * 1024
        ),
        name="gather_steps",
    )(dense, cotangent, node_inputs)


def body(cotangent, node_inputs, tiles, tile_rows, tile_cols, tile_counts):
    nodes = lax.axis_size("row") * lax.axis_size("col") * cotangent.shape[0]
    fits = nodes * nodes * tiles.dtype.itemsize <= LOCAL_BYTES
    pairs = lax.axis_size("col") == 2 and lax.axis_size("sub") == 2
    whole_tiles = cotangent.shape[0] == tiles.shape[3] and tiles.shape[3] % 32 == 0
    chosen = local_body if fits and pairs and whole_tiles else exchange_body
    return chosen(cotangent, node_inputs, tiles, tile_rows, tile_cols, tile_counts)


def solution(mesh):
    in_specs = (
        P(("grp", "col", "row"), "sub"),
        P(("grp", "col", "row"), "sub"),
        P(("grp", "row"), "col", None, None, None),
        P(("grp", "row"), "col", None),
        P(("grp", "row"), "col", None),
        P(("grp", "row"), "col"),
    )
    out_specs = (P(("grp", "col", "row"), "sub"), P("grp", "sub"))
    return jax.shard_map(body, mesh=mesh, in_specs=in_specs, out_specs=out_specs, check_vma=False)
```

```python
import functools

import jax
import jax.numpy as jnp
from jax import lax
from jax.experimental import pallas as pl
from jax.experimental.pallas import tpu as pltpu
from jax.sharding import PartitionSpec as P

PROP_STEPS = 4


teleport = 0.1

MESH = pl.DeviceIdType.MESH
LOCAL_BYTES = 8 * 1024 * 1024
PIECES = 2


def tile_products(stacked, live_tiles, own_rows, own_cols, block_tiles):
    chosen = jnp.take(stacked, own_cols, axis=0)
    products = jnp.einsum("sij,sjf->sif", live_tiles, chosen, preferred_element_type=jnp.float32)
    return jax.ops.segment_sum(products, own_rows, num_segments=block_tiles)


def exchange_body(cotangent, node_inputs, tiles, tile_rows, tile_cols, tile_counts):
    own_tiles = tiles[0, 0]
    own_rows = tile_rows[0, 0]
    own_cols = tile_cols[0, 0]
    own_count = tile_counts[0, 0]
    piece_rows, half_width = cotangent.shape
    slot_count = own_tiles.shape[0]
    tile_size = own_tiles.shape[1]
    row_devices = lax.axis_size("row")
    block_tiles = row_devices * piece_rows // tile_size
    live_mask = (jnp.arange(slot_count) < own_count).astype(jnp.bfloat16)
    live_tiles = own_tiles * live_mask[:, None, None]
    adjoint = cotangent
    node_grad = jnp.zeros_like(cotangent)
    for iteration in range(PROP_STEPS):
        node_grad = node_grad + teleport * adjoint
        sent = adjoint.astype(jnp.bfloat16)
        gathered = lax.all_gather(sent, "col", axis=0, tiled=True)
        stacked = gathered.reshape(-1, tile_size, half_width)
        partial_value = tile_products(stacked, live_tiles, own_rows, own_cols, block_tiles)
        rounded = lax.optimization_barrier(
            partial_value.reshape(block_tiles * tile_size, half_width).astype(jnp.bfloat16)
        )
        received = lax.all_to_all(
            rounded.reshape(row_devices, piece_rows, half_width),
            "row",
            split_axis=0,
            concat_axis=0,
            tiled=True,
        )
        summed = jnp.sum(received.astype(jnp.float32), axis=0)
        adjoint = (1.0 - teleport) * summed
    node_grad = node_grad + adjoint
    full_inputs = lax.all_gather(node_inputs, "sub", axis=1, tiled=True)
    terms = jnp.dot(full_inputs.astype(jnp.float32).T, node_grad, precision=lax.Precision.HIGHEST)
    weight_grad = lax.psum(terms, ("row", "col"))
    return (node_grad, weight_grad)


def densify_kernel(
    chunk, rows_hbm, cols_hbm, count_ref, tiles_ref, out_ref, rows_ref, cols_ref, slots, totals, index_sems, sems
):
    slot_count, half, tile = slots.shape
    block_tiles = out_ref.shape[0] // half
    input_tiles = out_ref.shape[1] // tile
    first = pl.multiple_of(lax.axis_index("sub") * half, half)
    count = count_ref[0, 0]
    indices = [
        pltpu.make_async_copy(rows_hbm, rows_ref, index_sems.at[0]),
        pltpu.make_async_copy(cols_hbm, cols_ref, index_sems.at[1]),
    ]
    for copy in indices:
        copy.start()
    copies = []
    for k in range(slot_count // chunk):
        copies.append(
            pltpu.make_async_copy(
                tiles_ref.at[0, 0, pl.ds(k * chunk, chunk), pl.ds(first, half), :],
                slots.at[pl.ds(k * chunk, chunk)],
                sems.at[k],
            )
        )
        copies[-1].start()
    totals[...] = jnp.zeros_like(totals)
    for copy in indices:
        copy.wait()

    def add_slot(slot, carry):
        place = rows_ref[0, 0, slot] * input_tiles + cols_ref[0, 0, slot]
        totals[place] += slots[slot].astype(jnp.float32)
        return carry

    for k in range(slot_count // chunk):
        copies[k].wait()
        lax.fori_loop(k * chunk, jnp.minimum(count, (k + 1) * chunk), add_slot, 0)
    for b in range(block_tiles):
        for t in range(input_tiles):
            out_ref[b * half : (b + 1) * half, t * tile : (t + 1) * tile] = totals[b * input_tiles + t].astype(
                jnp.bfloat16
            )


def gather_kernel(
    n_row,
    dense_ref,
    cot_ref,
    inputs_ref,
    grad_ref,
    weight_ref,
    mat,
    states,
    feats,
    total,
    sem_send,
    sem_z,
    sem_x,
    sem_sib,
):
    c = lax.axis_index("col")
    r = lax.axis_index("row")
    h = lax.axis_index("sub")
    oc = 1 - c
    oh = 1 - h
    piece = cot_ref.shape[0]
    half = piece // 2
    span = dense_ref.shape[0] // PIECES
    has_up = r < n_row - 1
    has_down = r > 0
    up = {"row": r + 1}
    down = {"row": r - 1}
    across = {"col": oc}
    sibling = {"sub": oh}

    def place(kind, col, row, core, p):
        if kind == 0:
            return states.at[0, row, pl.ds(pl.multiple_of(col * piece, piece), piece), :]
        if kind == 1:
            return mat.at[col, core, row, pl.ds(pl.multiple_of(p * span, span), span), :]
        return feats.at[col, core, row]

    def remote(kind, col, row, core, p, link, sems, device):
        ref = place(kind, col, row, core, p)
        slot = (0, 1 + p, 1 + PIECES)[kind]
        recv = sems.at[slot, row] if link < 3 else sems.at[slot, col, row]
        return pltpu.make_async_remote_copy(
            src_ref=ref,
            dst_ref=ref,
            send_sem=sem_send.at[slot, link, col, row],
            recv_sem=recv,
            device_id=device,
            device_id_type=MESH,
        )

    def to_up(kind, row, p=0):
        return remote(kind, c, row, h, p, 0, sem_z, up)

    def to_down(kind, row, p=0):
        return remote(kind, c, row, h, p, 1, sem_z, down)

    def to_across(kind, row, p=0):
        return remote(kind, c, row, h, p, 2, sem_x, across)

    def to_sibling(kind, col, row, p=0):
        return remote(kind, col, row, h, p, 3, sem_sib, sibling)

    def from_z(kind, row, p=0):
        return remote(kind, c, row, h, p, 0, sem_z, across)

    def from_across(kind, row, p=0):
        return remote(kind, oc, row, h, p, 2, sem_x, across)

    def from_sibling(kind, col, row, p=0):
        return remote(kind, col, row, oh, p, 3, sem_sib, sibling)

    def each_piece(act):
        def at_piece(p, carry):
            act(p)
            return carry

        lax.fori_loop(0, PIECES, at_piece, 0)

    barrier = pltpu.get_barrier_semaphore()
    pl.semaphore_signal(barrier, inc=1, device_id=across, device_id_type=MESH)
    pl.semaphore_signal(barrier, inc=1, device_id=sibling, device_id_type=MESH)

    @pl.when(has_up)
    def _():
        pl.semaphore_signal(barrier, inc=1, device_id=up, device_id_type=MESH)

    @pl.when(has_down)
    def _():
        pl.semaphore_signal(barrier, inc=1, device_id=down, device_id_type=MESH)

    states[0, r, pl.ds(pl.multiple_of(c * piece, piece), piece), :] = cot_ref[...].astype(jnp.bfloat16)
    mat[c, h, r] = dense_ref[...]
    feats[c, h, r] = inputs_ref[...]

    pl.semaphore_wait(barrier, 2 + has_up.astype(jnp.int32) + has_down.astype(jnp.int32))

    def spread(kind, row, go_up, go_down, p=0):
        if go_up:
            @pl.when(has_up)
            def _():
                to_up(kind, row, p).start()
        if go_down:
            @pl.when(has_down)
            def _():
                to_down(kind, row, p).start()
        if kind < 2:
            to_across(kind, row, p).start()
        if kind > 0:
            to_sibling(kind, c, row, p).start()

    def from_both(kind, d, p=0):
        @pl.when(r >= d)
        def _():
            from_z(kind, r - d, p).wait_recv()
            spread(kind, r - d, True, False, p)

        @pl.when(r + d < n_row)
        def _():
            from_z(kind, r + d, p).wait_recv()
            spread(kind, r + d, False, True, p)

    def crossed(kind, row, p=0):
        from_across(kind, row, p).wait_recv()
        if kind > 0:
            to_sibling(kind, oc, row, p).start()

    def crossed_both(d):
        if d == 0:
            crossed(0, r)
            each_piece(lambda p: crossed(1, r, p))
            return

        @pl.when(r >= d)
        def _():
            crossed(0, r - d)

        @pl.when(r + d < n_row)
        def _():
            crossed(0, r + d)

        def at_piece(p):
            @pl.when(r >= d)
            def _():
                crossed(1, r - d, p)

            @pl.when(r + d < n_row)
            def _():
                crossed(1, r + d, p)

        each_piece(at_piece)

    spread(0, r, True, True)
    each_piece(lambda p: spread(1, r, True, True, p))
    spread(2, r, True, True)
    for d in range(1, n_row):
        from_both(0, d)
        each_piece(lambda p: from_both(1, d, p))
        from_both(2, d)
        if d == 1:
            crossed_both(0)
    for row in range(n_row):
        to_across(2, row).start()
    for d in range(1, n_row):
        crossed_both(d)

    for col in range(2):
        for row in range(n_row):
            each_piece(lambda p: from_sibling(1, col, row, p).wait_recv())

    for step in range(PROP_STEPS):
        now = 0 if step == 0 else 1 + (step - 1) % 2
        later = 1 + step % 2
        last = step == PROP_STEPS - 1
        if last:
            for row in range(n_row):
                crossed(2, row)

        def block(index):
            col, core = index // 2, index % 2
            out = jnp.dot(mat[col, core, 0], states[now, 0], preferred_element_type=jnp.float32)
            for row in range(1, n_row):
                out += jnp.dot(mat[col, core, row], states[now, row], preferred_element_type=jnp.float32)
            out = out * (1.0 - teleport)
            rows = pl.ds(index * half, half)
            for row in range(n_row):
                part = out[row * half : (row + 1) * half]
                if step == 0:
                    total[row, rows, :] = teleport * (states[0, row, rows, :].astype(jnp.float32) + part)
                elif last:
                    total[row, rows, :] += part
                else:
                    total[row, rows, :] += teleport * part
                if not last:
                    states[later, row, rows, :] = part.astype(jnp.bfloat16)

        for index in range(4):
            block(index)

    own = cot_ref[...]
    own_rows = pl.ds(pl.multiple_of(c * piece, piece), piece)
    grad = total[r, own_rows, :] + teleport * (own - own.astype(jnp.bfloat16).astype(jnp.float32))
    total[r, own_rows, :] = grad
    grad_ref[...] = grad

    for col in range(2):
        for row in range(n_row):
            from_sibling(2, col, row).wait_recv()

    width = inputs_ref.shape[1]
    for core in range(2):
        weight = jnp.zeros((width, cot_ref.shape[1]), jnp.float32)
        for col in range(2):
            for row in range(n_row):
                weight += lax.dot_general(
                    feats[col, core, row],
                    total[row, col * piece : (col + 1) * piece, :].astype(jnp.bfloat16),
                    (((0,), (0,)), ((), ())),
                    preferred_element_type=jnp.float32,
                )
        weight_ref[core * width : (core + 1) * width, :] = weight

    def sent(kind, row, p=0):
        to_across(kind, row, p).wait_send()

        @pl.when((row <= r) & has_up)
        def _():
            to_up(kind, row, p).wait_send()

        @pl.when((row >= r) & has_down)
        def _():
            to_down(kind, row, p).wait_send()

        if kind > 0:
            for col in range(2):
                to_sibling(kind, col, row, p).wait_send()

    def all_sent(row, carry):
        sent(0, row)
        each_piece(lambda p: sent(1, row, p))
        sent(2, row)
        return carry

    lax.fori_loop(0, n_row, all_sent, 0)


def local_body(cotangent, node_inputs, tiles, tile_rows, tile_cols, tile_counts):
    piece, width = cotangent.shape
    slot_count, tile = tiles.shape[2], tiles.shape[3]
    n_row = lax.axis_size("row")
    half = tile // 2
    chunk = 8 if slot_count % 8 == 0 else slot_count
    hbm = pl.BlockSpec(memory_space=pltpu.HBM)
    smem = pl.BlockSpec(memory_space=pltpu.SMEM)
    vmem = pl.BlockSpec(memory_space=pltpu.VMEM)
    dense = pl.pallas_call(
        functools.partial(densify_kernel, chunk),
        out_shape=jax.ShapeDtypeStruct((n_row * half, 2 * tile), jnp.bfloat16),
        in_specs=[hbm, hbm, smem, hbm],
        out_specs=vmem,
        scratch_shapes=[
            pltpu.SMEM(tile_rows.shape, jnp.int32),
            pltpu.SMEM(tile_cols.shape, jnp.int32),
            pltpu.VMEM((slot_count, half, tile), jnp.bfloat16),
            pltpu.VMEM((n_row * 2, half, tile), jnp.float32),
            pltpu.SemaphoreType.DMA((2,)),
            pltpu.SemaphoreType.DMA((slot_count // chunk,)),
        ],
        compiler_params=pltpu.CompilerParams(vmem_limit_bytes=16 * 1024 * 1024),
        name="densify",
    )(tile_rows, tile_cols, tile_counts, tiles)
    return pl.pallas_call(
        functools.partial(gather_kernel, n_row),
        out_shape=(
            jax.ShapeDtypeStruct((piece, width), jnp.float32),
            jax.ShapeDtypeStruct((2 * node_inputs.shape[1], width), jnp.float32),
        ),
        in_specs=[vmem, vmem, vmem],
        out_specs=(vmem, vmem),
        scratch_shapes=[
            pltpu.VMEM((2, 2, n_row, n_row * half, 2 * tile), jnp.bfloat16),
            pltpu.VMEM((3, n_row, 2 * piece, width), jnp.bfloat16),
            pltpu.VMEM((2, 2, n_row, piece, node_inputs.shape[1]), jnp.bfloat16),
            pltpu.VMEM((n_row, 2 * piece, width), jnp.float32),
            pltpu.SemaphoreType.DMA((2 + PIECES, 4, 2, n_row)),
            pltpu.SemaphoreType.DMA((2 + PIECES, n_row)),
            pltpu.SemaphoreType.DMA((2 + PIECES, n_row)),
            pltpu.SemaphoreType.DMA((2 + PIECES, 2, n_row)),
        ],
        compiler_params=pltpu.CompilerParams(
            collective_id=0, has_side_effects=True, vmem_limit_bytes=32 * 1024 * 1024
        ),
        name="gather_steps",
    )(dense, cotangent, node_inputs)


def body(cotangent, node_inputs, tiles, tile_rows, tile_cols, tile_counts):
    nodes = lax.axis_size("row") * lax.axis_size("col") * cotangent.shape[0]
    fits = nodes * nodes * tiles.dtype.itemsize <= LOCAL_BYTES
    pairs = lax.axis_size("col") == 2 and lax.axis_size("sub") == 2
    whole_tiles = cotangent.shape[0] == tiles.shape[3] and tiles.shape[3] % 32 == 0
    chosen = local_body if fits and pairs and whole_tiles else exchange_body
    return chosen(cotangent, node_inputs, tiles, tile_rows, tile_cols, tile_counts)


def solution(mesh):
    in_specs = (
        P(("grp", "col", "row"), "sub"),
        P(("grp", "col", "row"), "sub"),
        P(("grp", "row"), "col", None, None, None),
        P(("grp", "row"), "col", None),
        P(("grp", "row"), "col", None),
        P(("grp", "row"), "col"),
    )
    out_specs = (P(("grp", "col", "row"), "sub"), P("grp", "sub"))
    return jax.shard_map(body, mesh=mesh, in_specs=in_specs, out_specs=out_specs, check_vma=False)
```

```python
import functools

import jax
import jax.numpy as jnp
from jax import lax
from jax.experimental import pallas as pl
from jax.experimental.pallas import tpu as pltpu
from jax.sharding import PartitionSpec as P

PROP_STEPS = 4


teleport = 0.1

MESH = pl.DeviceIdType.MESH
LOCAL_BYTES = 8 * 1024 * 1024
PIECES = 2


def tile_products(stacked, live_tiles, own_rows, own_cols, block_tiles):
    chosen = jnp.take(stacked, own_cols, axis=0)
    products = jnp.einsum("sij,sjf->sif", live_tiles, chosen, preferred_element_type=jnp.float32)
    return jax.ops.segment_sum(products, own_rows, num_segments=block_tiles)


def exchange_body(cotangent, node_inputs, tiles, tile_rows, tile_cols, tile_counts):
    own_tiles = tiles[0, 0]
    own_rows = tile_rows[0, 0]
    own_cols = tile_cols[0, 0]
    own_count = tile_counts[0, 0]
    piece_rows, half_width = cotangent.shape
    slot_count = own_tiles.shape[0]
    tile_size = own_tiles.shape[1]
    row_devices = lax.axis_size("row")
    block_tiles = row_devices * piece_rows // tile_size
    live_mask = (jnp.arange(slot_count) < own_count).astype(jnp.bfloat16)
    live_tiles = own_tiles * live_mask[:, None, None]
    adjoint = cotangent
    node_grad = jnp.zeros_like(cotangent)
    for iteration in range(PROP_STEPS):
        node_grad = node_grad + teleport * adjoint
        sent = adjoint.astype(jnp.bfloat16)
        gathered = lax.all_gather(sent, "col", axis=0, tiled=True)
        stacked = gathered.reshape(-1, tile_size, half_width)
        partial_value = tile_products(stacked, live_tiles, own_rows, own_cols, block_tiles)
        rounded = lax.optimization_barrier(
            partial_value.reshape(block_tiles * tile_size, half_width).astype(jnp.bfloat16)
        )
        received = lax.all_to_all(
            rounded.reshape(row_devices, piece_rows, half_width),
            "row",
            split_axis=0,
            concat_axis=0,
            tiled=True,
        )
        summed = jnp.sum(received.astype(jnp.float32), axis=0)
        adjoint = (1.0 - teleport) * summed
    node_grad = node_grad + adjoint
    full_inputs = lax.all_gather(node_inputs, "sub", axis=1, tiled=True)
    terms = jnp.dot(full_inputs.astype(jnp.float32).T, node_grad, precision=lax.Precision.HIGHEST)
    weight_grad = lax.psum(terms, ("row", "col"))
    return (node_grad, weight_grad)


def densify_kernel(
    chunk, rows_hbm, cols_hbm, count_ref, tiles_ref, out_ref, rows_ref, cols_ref, slots, totals, index_sems, sems
):
    slot_count, half, tile = slots.shape
    block_tiles = out_ref.shape[0] // half
    input_tiles = out_ref.shape[1] // tile
    first = pl.multiple_of(lax.axis_index("sub") * half, half)
    count = count_ref[0, 0]
    indices = [
        pltpu.make_async_copy(rows_hbm, rows_ref, index_sems.at[0]),
        pltpu.make_async_copy(cols_hbm, cols_ref, index_sems.at[1]),
    ]
    for copy in indices:
        copy.start()
    copies = []
    for k in range(slot_count // chunk):
        copies.append(
            pltpu.make_async_copy(
                tiles_ref.at[0, 0, pl.ds(k * chunk, chunk), pl.ds(first, half), :],
                slots.at[pl.ds(k * chunk, chunk)],
                sems.at[k],
            )
        )
        copies[-1].start()
    totals[...] = jnp.zeros_like(totals)
    for copy in indices:
        copy.wait()

    def add_slot(slot, carry):
        place = rows_ref[0, 0, slot] * input_tiles + cols_ref[0, 0, slot]
        totals[place] += slots[slot].astype(jnp.float32)
        return carry

    for k in range(slot_count // chunk):
        copies[k].wait()
        lax.fori_loop(k * chunk, jnp.minimum(count, (k + 1) * chunk), add_slot, 0)
    for b in range(block_tiles):
        for t in range(input_tiles):
            out_ref[b * half : (b + 1) * half, t * tile : (t + 1) * tile] = totals[b * input_tiles + t].astype(
                jnp.bfloat16
            )


def gather_kernel(
    n_row,
    dense_ref,
    cot_ref,
    inputs_ref,
    grad_ref,
    weight_ref,
    mat,
    states,
    feats,
    total,
    sem_send,
    sem_z,
    sem_x,
    sem_sib,
):
    c = lax.axis_index("col")
    r = lax.axis_index("row")
    h = lax.axis_index("sub")
    oc = 1 - c
    oh = 1 - h
    piece = cot_ref.shape[0]
    half = piece // 2
    span = dense_ref.shape[0] // PIECES
    has_up = r < n_row - 1
    has_down = r > 0
    up = {"row": r + 1}
    down = {"row": r - 1}
    across = {"col": oc}
    sibling = {"sub": oh}

    def place(kind, col, row, core, p):
        if kind == 0:
            return states.at[0, row, pl.ds(pl.multiple_of(col * piece, piece), piece), :]
        if kind == 1:
            return mat.at[col, core, row, pl.ds(pl.multiple_of(p * span, span), span), :]
        return feats.at[col, core, row]

    def remote(kind, col, row, core, p, link, sems, device):
        ref = place(kind, col, row, core, p)
        slot = (0, 1 + p, 1 + PIECES)[kind]
        recv = sems.at[slot, row] if link < 3 else sems.at[slot, col, row]
        return pltpu.make_async_remote_copy(
            src_ref=ref,
            dst_ref=ref,
            send_sem=sem_send.at[slot, link, col, row],
            recv_sem=recv,
            device_id=device,
            device_id_type=MESH,
        )

    def to_up(kind, row, p=0):
        return remote(kind, c, row, h, p, 0, sem_z, up)

    def to_down(kind, row, p=0):
        return remote(kind, c, row, h, p, 1, sem_z, down)

    def to_across(kind, row, p=0):
        return remote(kind, c, row, h, p, 2, sem_x, across)

    def to_sibling(kind, col, row, p=0):
        return remote(kind, col, row, h, p, 3, sem_sib, sibling)

    def from_z(kind, row, p=0):
        return remote(kind, c, row, h, p, 0, sem_z, across)

    def from_across(kind, row, p=0):
        return remote(kind, oc, row, h, p, 2, sem_x, across)

    def from_sibling(kind, col, row, p=0):
        return remote(kind, col, row, oh, p, 3, sem_sib, sibling)

    def each_piece(act):
        def at_piece(p, carry):
            act(p)
            return carry

        lax.fori_loop(0, PIECES, at_piece, 0)

    barrier = pltpu.get_barrier_semaphore()
    pl.semaphore_signal(barrier, inc=1, device_id=across, device_id_type=MESH)
    pl.semaphore_signal(barrier, inc=1, device_id=sibling, device_id_type=MESH)

    @pl.when(has_up)
    def _():
        pl.semaphore_signal(barrier, inc=1, device_id=up, device_id_type=MESH)

    @pl.when(has_down)
    def _():
        pl.semaphore_signal(barrier, inc=1, device_id=down, device_id_type=MESH)

    states[0, r, pl.ds(pl.multiple_of(c * piece, piece), piece), :] = cot_ref[...].astype(jnp.bfloat16)
    mat[c, h, r] = dense_ref[...]
    feats[c, h, r] = inputs_ref[...]

    pl.semaphore_wait(barrier, 2 + has_up.astype(jnp.int32) + has_down.astype(jnp.int32))

    def spread(kind, row, go_up, go_down, p=0):
        if go_up:
            @pl.when(has_up)
            def _():
                to_up(kind, row, p).start()
        if go_down:
            @pl.when(has_down)
            def _():
                to_down(kind, row, p).start()
        if kind < 2:
            to_across(kind, row, p).start()
        if kind > 0:
            to_sibling(kind, c, row, p).start()

    def from_both(kind, d, p=0):
        @pl.when(r >= d)
        def _():
            from_z(kind, r - d, p).wait_recv()
            spread(kind, r - d, True, False, p)

        @pl.when(r + d < n_row)
        def _():
            from_z(kind, r + d, p).wait_recv()
            spread(kind, r + d, False, True, p)

    def crossed(kind, row, p=0):
        from_across(kind, row, p).wait_recv()
        if kind > 0:
            to_sibling(kind, oc, row, p).start()

    def crossed_both(d):
        if d == 0:
            crossed(0, r)
            each_piece(lambda p: crossed(1, r, p))
            return

        @pl.when(r >= d)
        def _():
            crossed(0, r - d)

        @pl.when(r + d < n_row)
        def _():
            crossed(0, r + d)

        def at_piece(p):
            @pl.when(r >= d)
            def _():
                crossed(1, r - d, p)

            @pl.when(r + d < n_row)
            def _():
                crossed(1, r + d, p)

        each_piece(at_piece)

    spread(0, r, True, True)
    each_piece(lambda p: spread(1, r, True, True, p))
    spread(2, r, True, True)
    for d in range(1, n_row):
        from_both(0, d)
        each_piece(lambda p: from_both(1, d, p))
        if d > 1:
            from_both(2, d - 1)
    from_both(2, n_row - 1)
    crossed_both(0)
    for row in range(n_row):
        to_across(2, row).start()
    for d in range(1, n_row):
        crossed_both(d)

    for col in range(2):
        for row in range(n_row):
            each_piece(lambda p: from_sibling(1, col, row, p).wait_recv())

    for step in range(PROP_STEPS):
        now = 0 if step == 0 else 1 + (step - 1) % 2
        later = 1 + step % 2
        last = step == PROP_STEPS - 1
        if last:
            for row in range(n_row):
                crossed(2, row)

        def block(index):
            col, core = index // 2, index % 2
            out = jnp.dot(mat[col, core, 0], states[now, 0], preferred_element_type=jnp.float32)
            for row in range(1, n_row):
                out += jnp.dot(mat[col, core, row], states[now, row], preferred_element_type=jnp.float32)
            out = out * (1.0 - teleport)
            rows = pl.ds(index * half, half)
            for row in range(n_row):
                part = out[row * half : (row + 1) * half]
                if step == 0:
                    total[row, rows, :] = teleport * (states[0, row, rows, :].astype(jnp.float32) + part)
                elif last:
                    total[row, rows, :] += part
                else:
                    total[row, rows, :] += teleport * part
                if not last:
                    states[later, row, rows, :] = part.astype(jnp.bfloat16)

        for index in range(4):
            block(index)

    own = cot_ref[...]
    own_rows = pl.ds(pl.multiple_of(c * piece, piece), piece)
    grad = total[r, own_rows, :] + teleport * (own - own.astype(jnp.bfloat16).astype(jnp.float32))
    total[r, own_rows, :] = grad
    grad_ref[...] = grad

    for col in range(2):
        for row in range(n_row):
            from_sibling(2, col, row).wait_recv()

    width = inputs_ref.shape[1]
    for core in range(2):
        weight = jnp.zeros((width, cot_ref.shape[1]), jnp.float32)
        for col in range(2):
            for row in range(n_row):
                weight += lax.dot_general(
                    feats[col, core, row],
                    total[row, col * piece : (col + 1) * piece, :].astype(jnp.bfloat16),
                    (((0,), (0,)), ((), ())),
                    preferred_element_type=jnp.float32,
                )
        weight_ref[core * width : (core + 1) * width, :] = weight

    def sent(kind, row, p=0):
        to_across(kind, row, p).wait_send()

        @pl.when((row <= r) & has_up)
        def _():
            to_up(kind, row, p).wait_send()

        @pl.when((row >= r) & has_down)
        def _():
            to_down(kind, row, p).wait_send()

        if kind > 0:
            for col in range(2):
                to_sibling(kind, col, row, p).wait_send()

    def all_sent(row, carry):
        sent(0, row)
        each_piece(lambda p: sent(1, row, p))
        sent(2, row)
        return carry

    lax.fori_loop(0, n_row, all_sent, 0)


def local_body(cotangent, node_inputs, tiles, tile_rows, tile_cols, tile_counts):
    piece, width = cotangent.shape
    slot_count, tile = tiles.shape[2], tiles.shape[3]
    n_row = lax.axis_size("row")
    half = tile // 2
    chunk = 8 if slot_count % 8 == 0 else slot_count
    hbm = pl.BlockSpec(memory_space=pltpu.HBM)
    smem = pl.BlockSpec(memory_space=pltpu.SMEM)
    vmem = pl.BlockSpec(memory_space=pltpu.VMEM)
    dense = pl.pallas_call(
        functools.partial(densify_kernel, chunk),
        out_shape=jax.ShapeDtypeStruct((n_row * half, 2 * tile), jnp.bfloat16),
        in_specs=[hbm, hbm, smem, hbm],
        out_specs=vmem,
        scratch_shapes=[
            pltpu.SMEM(tile_rows.shape, jnp.int32),
            pltpu.SMEM(tile_cols.shape, jnp.int32),
            pltpu.VMEM((slot_count, half, tile), jnp.bfloat16),
            pltpu.VMEM((n_row * 2, half, tile), jnp.float32),
            pltpu.SemaphoreType.DMA((2,)),
            pltpu.SemaphoreType.DMA((slot_count // chunk,)),
        ],
        compiler_params=pltpu.CompilerParams(vmem_limit_bytes=16 * 1024 * 1024),
        name="densify",
    )(tile_rows, tile_cols, tile_counts, tiles)
    return pl.pallas_call(
        functools.partial(gather_kernel, n_row),
        out_shape=(
            jax.ShapeDtypeStruct((piece, width), jnp.float32),
            jax.ShapeDtypeStruct((2 * node_inputs.shape[1], width), jnp.float32),
        ),
        in_specs=[vmem, vmem, vmem],
        out_specs=(vmem, vmem),
        scratch_shapes=[
            pltpu.VMEM((2, 2, n_row, n_row * half, 2 * tile), jnp.bfloat16),
            pltpu.VMEM((3, n_row, 2 * piece, width), jnp.bfloat16),
            pltpu.VMEM((2, 2, n_row, piece, node_inputs.shape[1]), jnp.bfloat16),
            pltpu.VMEM((n_row, 2 * piece, width), jnp.float32),
            pltpu.SemaphoreType.DMA((2 + PIECES, 4, 2, n_row)),
            pltpu.SemaphoreType.DMA((2 + PIECES, n_row)),
            pltpu.SemaphoreType.DMA((2 + PIECES, n_row)),
            pltpu.SemaphoreType.DMA((2 + PIECES, 2, n_row)),
        ],
        compiler_params=pltpu.CompilerParams(
            collective_id=0, has_side_effects=True, vmem_limit_bytes=32 * 1024 * 1024
        ),
        name="gather_steps",
    )(dense, cotangent, node_inputs)


def body(cotangent, node_inputs, tiles, tile_rows, tile_cols, tile_counts):
    nodes = lax.axis_size("row") * lax.axis_size("col") * cotangent.shape[0]
    fits = nodes * nodes * tiles.dtype.itemsize <= LOCAL_BYTES
    pairs = lax.axis_size("col") == 2 and lax.axis_size("sub") == 2
    whole_tiles = cotangent.shape[0] == tiles.shape[3] and tiles.shape[3] % 32 == 0
    chosen = local_body if fits and pairs and whole_tiles else exchange_body
    return chosen(cotangent, node_inputs, tiles, tile_rows, tile_cols, tile_counts)


def solution(mesh):
    in_specs = (
        P(("grp", "col", "row"), "sub"),
        P(("grp", "col", "row"), "sub"),
        P(("grp", "row"), "col", None, None, None),
        P(("grp", "row"), "col", None),
        P(("grp", "row"), "col", None),
        P(("grp", "row"), "col"),
    )
    out_specs = (P(("grp", "col", "row"), "sub"), P("grp", "sub"))
    return jax.shard_map(body, mesh=mesh, in_specs=in_specs, out_specs=out_specs, check_vma=False)
```
